32 devices in a mesh: px: 4 (over y, core), py: 8 (over z, x).
Axes of the slice: x: 2, y: 2, z: 4, core: 2. Of those that a mesh axis runs over, the one named last changes fastest.
Arguments:
- fine_residual: bfloat16 [131072, 256], P(('px', 'py')), may hold values from -6 to 6
- dest_owner: int32 [131072], P(('px', 'py')), may hold values from 0 to 31, as said below
- coarse_slot: int32 [131072], P(('px', 'py')), may hold values from 0 to 511, as said below
- ghost_slot: int32 [128, 32], P(('px', 'py')), may hold values from 0 to 511, as said below
- child_type: int32 [131072], P(('px', 'py')), may hold values from 0 to 7
- restrict_table: bfloat16 [8, 64, 64], replicated, may hold values from -0.75 to 0.75
- inverse_blocks: bfloat16 [16384, 4096], P(('px', 'py')), may hold values from -0.45 to 1.05
- face_table: bfloat16 [6, 64, 64], replicated, may hold values from -0.75 to 0.75
- face_coef: float32 [16], replicated, may hold values from 0.2 to 2
- coef_index: int32 [6, 16384], P(None, ('px', 'py')), may hold values from 0 to 15
- neighbours: int32 [6, 16384], P(None, ('px', 'py')), may hold values from 0 to 16383, as said below
Outputs:
- coarse_solution: float32 [16384, 256], P(('px', 'py'))
- fine_correction: bfloat16 [131072, 256], P(('px', 'py'))
The draws below stay inside these ranges and needn't reach their ends.
Inputs may be any that keep to these rules, and one draw needn't show every extreme that they name: `dest_owner`: the owner is the element's own device or a device one step away along py (same px index) or along px (same py index); every coarse element has exactly 8 fine children, with distinct child_type. `coarse_slot`: for an element whose parent lives on another device the value is below 32. `ghost_slot`: j = 0, 1, 2, 3 stands for the device one lower along py, one higher along py, one lower along px, one higher along px; a device's four lists hold distinct elements; each remote child of a device's coarse element is found in the list toward the child's device, at the row that its coarse_slot names; between two neighbouring devices at most 32 parents have children across, and some pair has exactly 32. `neighbours`: the element across a face lives on the same device or on a device one step away along py or along px, never outside the grid.
All inputs are finite; a program needn't handle non-finite values.
Results may differ from the reference program's by a relative error of at most 0.0073.
Values may be sent and summed in bfloat16 or wider, within the bound.
A program may use at most 64 MiB of HBM per device.

```python
import math
import jax
import jax.numpy as jnp

DOF = 64
RHS = 4
W = 256
NTYPE = 8
FACES = 6
KINDS = 16
F_DEV = 4096
C_DEV = 512
GHOST = 32
NF = 131072
NC = 16384
N_PX = 4
N_PY = 8
DEVICES = 32


def geometry(key):
    base = jax.random.fold_in(key, 7)
    device_ids = jnp.arange(DEVICES, dtype=jnp.int32)
    permuted = jax.vmap(lambda number: jax.random.permutation(jax.random.fold_in(base, number), C_DEV))(device_ids).astype(jnp.int32)
    shuffle_key = jax.random.fold_in(base, 3)
    shuffles = jax.vmap(lambda number: jax.random.permutation(jax.random.fold_in(shuffle_key, number), F_DEV))(device_ids).astype(jnp.int32)
    lowest = max(1, GHOST // 2)
    ghost_py = jax.random.randint(jax.random.fold_in(base, 5), (N_PX, N_PY), lowest, GHOST + 1, dtype=jnp.int32)
    ghost_px = jax.random.randint(jax.random.fold_in(base, 6), (N_PX, N_PY), lowest, GHOST + 1, dtype=jnp.int32)
    pick_first = jax.random.randint(jax.random.fold_in(base, 8), (), 0, N_PX, dtype=jnp.int32)
    pick_second = jax.random.randint(jax.random.fold_in(base, 9), (), 0, N_PY - 1, dtype=jnp.int32)
    ghost_py = ghost_py.at[pick_first, pick_second].set(GHOST)
    pick_third = jax.random.randint(jax.random.fold_in(base, 10), (), 0, N_PX - 1, dtype=jnp.int32)
    pick_fourth = jax.random.randint(jax.random.fold_in(base, 12), (), 0, N_PY, dtype=jnp.int32)
    ghost_px = ghost_px.at[pick_third, pick_fourth].set(GHOST)
    record = jnp.arange(F_DEV, dtype=jnp.int32)[None, :]
    parent_local = record // 8
    position_kind = record % 8
    group_id = parent_local // GHOST
    rank_id = parent_local % GHOST
    coord_first = (device_ids // N_PY)[:, None]
    coord_second = (device_ids % N_PY)[:, None]
    limit_zero = ghost_py[coord_first, jnp.maximum(coord_second - 1, 0)]
    limit_one = ghost_py[coord_first, coord_second]
    limit_two = ghost_px[jnp.maximum(coord_first - 1, 0), coord_second]
    limit_three = ghost_px[coord_first, coord_second]
    cross_zero = (group_id == 0) & (coord_second > 0) & (rank_id < limit_zero) & (position_kind >= 4)
    cross_one = (group_id == 1) & (coord_second < N_PY - 1) & (rank_id < limit_one) & (position_kind >= 4)
    cross_two = (group_id == 2) & (coord_first > 0) & (rank_id < limit_two) & (position_kind % 2 == 1)
    cross_three = (group_id == 3) & (coord_first < N_PX - 1) & (rank_id < limit_three) & (position_kind % 2 == 1)
    step_size = jnp.where(cross_zero, -1, jnp.where(cross_one, 1, jnp.where(cross_two, -N_PY, jnp.where(cross_three, N_PY, 0)))).astype(jnp.int32)
    owners = (device_ids[:, None] + step_size).astype(jnp.int32)
    remote = step_size != 0
    local_slot = jnp.take_along_axis(permuted, jnp.broadcast_to(parent_local, (DEVICES, F_DEV)), axis=1)
    slots = jnp.where(remote, jnp.broadcast_to(rank_id, (DEVICES, F_DEV)), local_slot).astype(jnp.int32)
    types = jnp.broadcast_to(position_kind, (DEVICES, F_DEV)).astype(jnp.int32)
    owners = jnp.take_along_axis(owners, shuffles, axis=1)
    slots = jnp.take_along_axis(slots, shuffles, axis=1)
    types = jnp.take_along_axis(types, shuffles, axis=1)
    ghost_lists = permuted[:, :4 * GHOST].reshape(DEVICES * 4, GHOST).astype(jnp.int32)
    return (owners.reshape(NF), slots.reshape(NF), types.reshape(NF), ghost_lists)


def draw_dest_owner(key, part):
    return geometry(key)[0]


def draw_coarse_slot(key, part):
    return geometry(key)[1]


def draw_child_type(key, part):
    return geometry(key)[2]


def draw_ghost_slot(key, part):
    return geometry(key)[3]


def draw_inverse_blocks(key, part):
    noise = jnp.clip(jax.random.normal(key, (NC, DOF, DOF), jnp.float32), -6.0, 6.0)
    identity = jnp.eye(DOF, dtype=jnp.float32)
    blocks = 0.6 * identity[None, :, :] + 0.075 * noise
    return blocks.reshape(NC, DOF * DOF).astype(jnp.bfloat16)


def draw_neighbours(key, part):
    cells = jnp.arange(NC, dtype=jnp.int32)
    owners = cells // C_DEV
    coord_first = (owners // N_PY)[None, :]
    coord_second = (owners % N_PY)[None, :]
    face_ids = jnp.arange(FACES, dtype=jnp.int32)[:, None]
    crossing = jax.random.randint(jax.random.fold_in(key, 11), (FACES, NC), 0, 2, dtype=jnp.int32) == 1
    step_second = jnp.where(face_ids == 0, -1, jnp.where(face_ids == 1, 1, 0))
    step_first = jnp.where(face_ids == 2, -1, jnp.where(face_ids == 3, 1, 0))
    inside = (coord_second + step_second >= 0) & (coord_second + step_second < N_PY) & (coord_first + step_first >= 0) & (coord_first + step_first < N_PX)
    moved = crossing & inside
    target = owners[None, :] + jnp.where(moved, step_first * N_PY + step_second, 0)
    slot_pick = jax.random.randint(jax.random.fold_in(key, 12), (FACES, NC), 0, C_DEV, dtype=jnp.int32)
    return (target * C_DEV + slot_pick).astype(jnp.int32)


def place_ends(result, rng, least, high):
    place = [jax.random.randint(jax.random.fold_in(rng, axis), (), 0, length) for axis, length in enumerate(result.shape)]
    widest = result.shape.index(max(result.shape))
    next_to = place[:widest] + [(place[widest] + 1) % result.shape[widest]] + place[widest + 1:]
    return result.at[tuple(place)].set(least).at[tuple(next_to)].set(high)


def shard_levels(own_key, dims, pieces, low, largest):
    gain, own = 1.0, jax.random.fold_in(own_key, 6)
    for axis_at, parts in pieces:
        heights = jnp.exp(jax.random.uniform(jax.random.fold_in(own, axis_at), (parts,), jnp.float32, low / len(pieces), largest / len(pieces)))
        gain = gain * jnp.repeat(heights, dims[axis_at] // parts).reshape([-1 if axis == axis_at else 1 for axis in range(len(dims))])
    return gain


def normal_values(rng, dims, scale, most, split=(), kind=jnp.bfloat16):
    entries = jax.random.normal(rng, dims, jnp.float32) * scale
    if len(split) > 0:
        entries = shard_levels(rng, dims, split, -0.22, 0.18) * entries
    return jnp.clip(entries, min=-most, max=most).astype(kind)


def setup_inputs(seed: int = 0) -> dict:
    arg_keys = jax.random.split(jax.random.key(seed), 12)
    return {
        "fine_residual": normal_values(arg_keys[0], (NF, W), 1.0, 6.0, ((0, 32),)),
        "dest_owner": draw_dest_owner(jax.random.fold_in(arg_keys[11], 71), 0),
        "coarse_slot": draw_coarse_slot(jax.random.fold_in(arg_keys[11], 71), 0),
        "ghost_slot": draw_ghost_slot(jax.random.fold_in(arg_keys[11], 71), 0),
        "child_type": draw_child_type(jax.random.fold_in(arg_keys[11], 71), 0),
        "restrict_table": normal_values(arg_keys[5], (NTYPE, DOF, DOF), DOF ** -0.5, 0.75),
        "inverse_blocks": draw_inverse_blocks(jax.random.fold_in(arg_keys[11], 71), 0),
        "face_table": normal_values(arg_keys[7], (FACES, DOF, DOF), DOF ** -0.5, 0.75),
        "face_coef": jnp.clip(jnp.exp(jax.random.uniform(arg_keys[8], (KINDS,), jnp.float32, math.log(0.2), math.log(2.0))), 0.2, 2.0),
        "coef_index": place_ends(jax.random.randint(arg_keys[9], (FACES, NC), 0, KINDS), jax.random.fold_in(arg_keys[9], 1), 0, KINDS - 1).astype(jnp.int32),
        "neighbours": draw_neighbours(jax.random.fold_in(arg_keys[11], 71), 0),
    }


omega = 0.5


def typed_apply(blocks, child_type, matrices):
    item_count = blocks.shape[0]
    shaped = blocks.reshape(item_count, RHS, DOF).astype(jnp.float32)
    accum = jnp.zeros((item_count, RHS, DOF), jnp.float32)
    for type_id in range(NTYPE):
        product = jnp.einsum("nsj,ij->nsi", shaped, matrices[type_id].astype(jnp.float32))
        accum = accum + jnp.where((child_type == type_id)[:, None, None], product, jnp.float32(0.0))
    return accum.reshape(item_count, W)


def reference(fine_residual, dest_owner, coarse_slot, ghost_slot, child_type, restrict_table, inverse_blocks, face_table, face_coef, coef_index, neighbours):
    own_device = (jnp.arange(NF, dtype=jnp.int32) // F_DEV).astype(jnp.int32)
    offset = (dest_owner - own_device).astype(jnp.int32)
    is_local = offset == 0
    direction = jnp.where(offset == -1, 1, jnp.where(offset == 1, 0, jnp.where(offset < 0, 3, 2))).astype(jnp.int32)
    ghost_row = jnp.where(is_local, 0, coarse_slot).astype(jnp.int32)
    ghost_pick = ghost_slot[(dest_owner * 4 + direction).astype(jnp.int32), ghost_row]
    parent_slot = jnp.where(is_local, coarse_slot, ghost_pick).astype(jnp.int32)
    parent = (dest_owner * C_DEV + parent_slot).astype(jnp.int32)
    contrib = typed_apply(fine_residual, child_type, restrict_table).astype(jnp.bfloat16)
    coarse_rhs = jax.ops.segment_sum(contrib.astype(jnp.float32), parent, num_segments=NC).astype(jnp.bfloat16)
    inverse = inverse_blocks.reshape(NC, DOF, DOF).astype(jnp.float32)
    first_sweep = jnp.einsum("cij,csj->csi", inverse, coarse_rhs.reshape(NC, RHS, DOF).astype(jnp.float32))
    first_sweep = first_sweep.reshape(NC, W).astype(jnp.bfloat16)
    face_scale = face_coef[coef_index]
    coupled = jnp.zeros((NC, RHS, DOF), jnp.float32)
    for face_id in range(FACES):
        beside = first_sweep[neighbours[face_id]].reshape(NC, RHS, DOF).astype(jnp.float32)
        product = jnp.einsum("csj,ij->csi", beside, face_table[face_id].astype(jnp.float32))
        coupled = coupled + face_scale[face_id][:, None, None] * product
    coupled = coupled.astype(jnp.bfloat16)
    correction = jnp.einsum("cij,csj->csi", inverse, coupled.astype(jnp.float32)).reshape(NC, W)
    coarse_solution = first_sweep.astype(jnp.float32) - omega * correction
    answer = coarse_solution.astype(jnp.bfloat16)
    fetched = answer[parent]
    fine_correction = typed_apply(fetched, child_type, jnp.transpose(restrict_table, (0, 2, 1))).astype(jnp.bfloat16)
    return coarse_solution, fine_correction
```

```python
import functools

import jax
import jax.numpy as jnp
from jax import lax
from jax.experimental import pallas as pl
from jax.experimental.pallas import tpu as pltpu
from jax.sharding import PartitionSpec as P

omega = 0.5
MESH = pl.DeviceIdType.MESH
f32 = jnp.float32
bf16 = jnp.bfloat16
i32 = jnp.int32


def iota(shape, dim):
    return lax.broadcasted_iota(i32, shape, dim)


def nn(a, b):
    return lax.dot_general(a, b, (((1,), (0,)), ((), ())), preferred_element_type=f32)


def nt(a, b):
    return lax.dot_general(a, b, (((1,), (1,)), ((), ())), preferred_element_type=f32)


def onehot(mask):
    return jnp.where(mask, f32(1.0), f32(0.0)).astype(bf16)


def tiler(width, order):
    return onehot(lax.rem(iota((width, order), 0), order) == iota((width, order), 1))


def block_diagonal(matrix, width, flipped):
    order = matrix.shape[0]
    spread = tiler(width, order)
    if flipped:
        half = nt(spread, matrix)
    else:
        half = nn(spread, matrix)
    full = nt(half.astype(bf16), spread)
    same = lax.div(iota((width, width), 0), order) == lax.div(iota((width, width), 1), order)
    return jnp.where(same, full, f32(0.0)).astype(bf16)


def columns_of(row):
    parts = [
        jnp.transpose(jnp.broadcast_to(row[:, at : at + 128], (128, 128)))
        for at in range(0, row.shape[1], 128)
    ]
    return jnp.concatenate(parts, axis=0)


def target_rows(owner, slot, me, coarse, ghost):
    offset = owner - me
    direction = jnp.where(offset == -1, 0, jnp.where(offset == 1, 1, jnp.where(offset < 0, 2, 3)))
    return jnp.where(offset == 0, slot, coarse + direction * ghost + slot)


def typed_sum(rows, kinds, tables, width, count):
    wide = jnp.concatenate([kinds] * (width // 128), axis=1)
    rows = rows.astype(f32)
    total = None
    for kind in range(count):
        part = nn(
            jnp.where(wide == kind, rows, f32(0.0)).astype(bf16),
            tables[kind * width : (kind + 1) * width, :],
        )
        total = part if total is None else total + part
    return total


def restrict_kernel(
    geometry, fine_ref, owner_ref, slot_ref, kind_ref, table_ref, inverse_ref,
    local_ref, out_ref, turned_ref, tables, perm, total,
):
    coarse, ghost, width, order, kinds, n_py = geometry
    me = lax.axis_index("px") * n_py + lax.axis_index("py")
    step = pl.program_id(0)
    half = 8 * order

    @pl.when(step == 0)
    def _():
        for kind in range(kinds):
            tables[kind * width : (kind + 1) * width, :] = block_diagonal(
                table_ref[kind], width, True
            )
        at = iota((half, half), 0)
        perm[...] = onehot(
            iota((half, half), 1) == lax.rem(at, 8) * order + lax.div(at, 8)
        )
        total[...] = jnp.zeros_like(total)

    chunk = fine_ref.shape[0]
    for begin in range(0, chunk, 512):
        span = slice(begin, begin + 512)
        contrib = typed_sum(
            fine_ref[span, :], columns_of(kind_ref[:, span]), tables, width, kinds
        ).astype(bf16)
        target = target_rows(owner_ref[:, span], slot_ref[:, span], me, coarse, ghost)
        rows = coarse + 4 * ghost
        total[...] += nn(onehot(iota((rows, 512), 0) == target), contrib)

    halves = [
        nt(perm[...], inverse_ref[:, at * half : (at + 1) * half]).reshape(order, 8, coarse)
        for at in range(2)
    ]
    turned_ref[...] = jnp.concatenate(halves, axis=1).astype(bf16)

    @pl.when(step == pl.num_programs(0) - 1)
    def _():
        local_ref[...] = total[:coarse, :]
        out_ref[...] = total[coarse:, :].astype(bf16)


def coarse_kernel(
    geometry, local_ref, outgoing, ghost_row_ref, turned, face_ref, coef_ref, index_ref,
    neighbour_ref, solution_ref, returned,
    incoming, reply, xt, first_t, near, code, beside,
    ghost_send, ghost_recv, reply_send, reply_recv, halo_send, halo_recv,
):
    coarse, ghost, width, order, n_px, n_py, kinds = geometry
    rhs = width // order
    faces = face_ref.shape[0]
    px = lax.axis_index("px")
    py = lax.axis_index("py")
    me = px * n_py + py
    exists = [py > 0, py < n_py - 1, px > 0, px < n_px - 1]
    place = [(px, py - 1), (px, py + 1), (px - 1, py), (px + 1, py)]
    far = [(py > 1, (px, py - 2)), (py < n_py - 2, (px, py + 2))]

    for slot, there in enumerate(exists):
        @pl.when(jnp.logical_not(there))
        def _():
            near[slot + 1] = jnp.zeros((coarse, width), bf16)
            incoming[pl.ds(slot * ghost, ghost), :] = jnp.zeros((ghost, width), bf16)
            returned[pl.ds(slot * ghost, ghost), :] = jnp.zeros((ghost, width), bf16)

    barrier = pltpu.get_barrier_semaphore()
    everyone = list(zip(exists, place)) + far
    for there, where in everyone:
        @pl.when(there)
        def _():
            pl.semaphore_signal(barrier, inc=1, device_id=where, device_id_type=MESH)
    pl.semaphore_wait(barrier, sum(there.astype(i32) for there, _ in everyone))

    def lists(source, target, send, recv, at, to):
        return pltpu.make_async_remote_copy(
            src_ref=source.at[pl.ds(at * ghost, ghost)],
            dst_ref=target.at[pl.ds(to * ghost, ghost)],
            send_sem=send.at[at],
            recv_sem=recv.at[to],
            device_id=place[at],
            device_id_type=MESH,
        )

    def start_lists(source, target, send, recv):
        for at in range(4):
            @pl.when(exists[at])
            def _():
                lists(source, target, send, recv, at, at ^ 1).start()

    def finish_lists(source, target, send, recv):
        for at in range(4):
            @pl.when(exists[at])
            def _():
                lists(source, target, send, recv, at, at).wait_recv()
                lists(source, target, send, recv, at, at ^ 1).wait_send()

    start_lists(outgoing, incoming, ghost_send, ghost_recv)

    offset = lax.shift_right_logical(neighbour_ref[...], coarse.bit_length() - 1) - me
    slot = jnp.where(
        offset == 0, 0,
        jnp.where(offset == -1, 1, jnp.where(offset == 1, 2, jnp.where(offset < 0, 3, 4))),
    )
    codes = slot * coarse + (neighbour_ref[...] & (coarse - 1))
    for face in range(faces):
        code[face * coarse : (face + 1) * coarse, :] = columns_of(codes[face : face + 1, :])
    scales = jnp.zeros(index_ref.shape, f32)
    for kind in range(kinds):
        scales = jnp.where(index_ref[...] == kind, coef_ref[0, kind], scales)
    lists_onehot = onehot(iota((coarse, 4 * ghost), 0) == ghost_row_ref[...])
    pick_onehot = onehot(
        jnp.concatenate([columns_of(ghost_row_ref[...])] * (coarse // 128), axis=1)
        == iota((4 * ghost, coarse), 1)
    )

    finish_lists(outgoing, incoming, ghost_send, ghost_recv)
    rhs_rows = local_ref[...] + nn(lists_onehot, incoming[...])
    xt[...] = jnp.transpose(rhs_rows.astype(bf16).astype(f32))

    def sweep(tile):
        lanes = slice(tile * 128, (tile + 1) * 128)

        def body(block, sums):
            sums = list(sums)
            values = [
                xt[pl.ds(pl.multiple_of(s * order + block * 8, 8), 8), lanes] for s in range(rhs)
            ]
            for inner in range(8):
                at = block * 8 + inner
                matrix = turned[at, :, lanes].astype(f32)
                for s in range(rhs):
                    sums[s] = sums[s] + matrix * values[s][inner : inner + 1, :]
            return tuple(sums)

        start = tuple(jnp.zeros((order, 128), f32) for _ in range(rhs))
        return jnp.concatenate(lax.fori_loop(0, order // 8, body, start), axis=0)

    even = lax.rem(py, 2) == 0
    partner = jnp.where(even, 2, 1)
    beyond = 3 - partner
    partner_place = (px, jnp.where(even, py + 1, py - 1))
    relay_place = (px, jnp.where(even, py + 2, py - 2))
    relays = jnp.where(even, py + 2, n_py + 1 - py) < n_py
    gets_relay = jnp.where(even, py - 2, n_py - 3 - py) >= 0

    def halo(role, tile, source, target, where):
        rows = pl.ds(tile * 128, 128)
        return pltpu.make_async_remote_copy(
            src_ref=near.at[source, rows],
            dst_ref=near.at[target, rows],
            send_sem=halo_send.at[role, tile],
            recv_sem=halo_recv.at[role, tile],
            device_id=where,
            device_id_type=MESH,
        )

    def to_partner(tile):
        return halo(0, tile, 0, beyond, partner_place)

    def from_partner(tile):
        return halo(0, tile, 0, partner, partner_place)

    def onward(tile):
        return halo(1, tile, partner, beyond, relay_place)

    def from_relay(tile):
        return halo(1, tile, partner, beyond, relay_place)

    def lower(tile):
        return halo(2, tile, 0, 4, place[2])

    def upper(tile):
        return halo(3, tile, 0, 3, place[3])

    tiles = coarse // 128
    for tile in range(tiles):
        lanes = slice(tile * 128, (tile + 1) * 128)
        rounded = sweep(tile).astype(bf16).astype(f32)
        first_t[:, lanes] = rounded
        near[0, lanes, :] = jnp.transpose(rounded).astype(bf16)
        to_partner(tile).start()

        @pl.when(exists[2])
        def _():
            lower(tile).start()

        @pl.when(exists[3])
        def _():
            upper(tile).start()

    step_rows = 256
    steps = faces * coarse // step_rows

    def gather(block, begin, end, fresh):
        def body(step, _):
            rows = pl.ds(pl.multiple_of(step * step_rows, step_rows), step_rows)
            here = code[rows, :] - block * coarse
            lane = iota((step_rows, 128), 1)
            picks = jnp.concatenate(
                [onehot(here == lane + at * 128) for at in range(tiles)], axis=1
            )
            found = nn(picks, near[block])
            if fresh:
                beside[rows, :] = found
            else:
                beside[rows, :] += found
            return 0

        lax.fori_loop(begin, end, body, 0)

    for tile in range(tiles):
        from_partner(tile).wait_recv()

        @pl.when(relays)
        def _():
            onward(tile).start()
        gather(0, tile * steps // tiles, (tile + 1) * steps // tiles, True)
    gather(partner, 0, steps, False)

    @pl.when(exists[2])
    def _():
        for tile in range(tiles):
            halo(3, tile, 0, 3, place[2]).wait_recv()
    gather(3, 0, steps, False)

    @pl.when(exists[3])
    def _():
        for tile in range(tiles):
            halo(2, tile, 0, 4, place[3]).wait_recv()
    gather(4, 0, steps, False)

    @pl.when(gets_relay)
    def _():
        for tile in range(tiles):
            from_relay(tile).wait_recv()
    gather(beyond, 0, steps, False)

    coupled = jnp.zeros((width, coarse), f32)
    for face in range(faces):
        matrix = block_diagonal(face_ref[face], width, False)
        rows = slice(face * coarse, (face + 1) * coarse)
        coupled += nt(matrix, beside[rows, :].astype(bf16)) * scales[face : face + 1, :]
    xt[...] = coupled.astype(bf16).astype(f32)

    for tile in range(tiles):
        lanes = slice(tile * 128, (tile + 1) * 128)
        solved = first_t[:, lanes] - omega * sweep(tile)
        solution_ref[lanes, :] = jnp.transpose(solved)

    reply[...] = nn(pick_onehot, solution_ref[...].astype(bf16)).astype(bf16)
    start_lists(reply, returned, reply_send, reply_recv)
    for tile in range(tiles):
        to_partner(tile).wait_send()

        @pl.when(relays)
        def _():
            onward(tile).wait_send()

        @pl.when(exists[2])
        def _():
            lower(tile).wait_send()

        @pl.when(exists[3])
        def _():
            upper(tile).wait_send()
    finish_lists(reply, returned, reply_send, reply_recv)


def prolong_kernel(
    geometry, solution_ref, returned_ref, owner_ref, slot_ref, kind_ref, table_ref,
    out_solution_ref, fine_ref, tables, held,
):
    coarse, ghost, width, order, kinds, n_py = geometry
    me = lax.axis_index("px") * n_py + lax.axis_index("py")
    step = pl.program_id(0)

    @pl.when(step == 0)
    def _():
        for kind in range(kinds):
            tables[kind * width : (kind + 1) * width, :] = block_diagonal(
                table_ref[kind], width, False
            )
        held[:coarse, :] = solution_ref[...].astype(bf16)
        held[coarse:, :] = returned_ref[...]
        out_solution_ref[...] = solution_ref[...]

    rows = coarse + 4 * ghost
    target = columns_of(target_rows(owner_ref[...], slot_ref[...], me, coarse, ghost))
    lane = iota(target.shape, 1)
    picks = jnp.concatenate([onehot(target == lane + at) for at in range(0, rows, 128)], axis=1)
    fetched = nn(picks, held[...]).astype(bf16)
    fine_ref[...] = typed_sum(
        fetched, columns_of(kind_ref[...]), tables, width, kinds
    ).astype(bf16)


def shards(
    n_px, n_py,
    fine_residual, dest_owner, coarse_slot, ghost_slot, child_type, restrict_table,
    inverse_blocks, face_table, face_coef, coef_index, neighbours,
):
    fine, width = fine_residual.shape
    coarse = inverse_blocks.shape[0]
    ghost = ghost_slot.shape[1]
    kinds, order, _ = restrict_table.shape
    faces = face_table.shape[0]
    owner = dest_owner.reshape(1, fine)
    slot = coarse_slot.reshape(1, fine)
    kind = child_type.reshape(1, fine)
    whole = pl.BlockSpec(memory_space=pltpu.VMEM)
    grant = 48 * 1024 * 1024

    steps = order // 16
    chunk = fine // steps
    geometry = (coarse, ghost, width, order, kinds, n_py)
    row = pl.BlockSpec((1, chunk), lambda i: (0, i))
    local, outgoing, turned = pl.pallas_call(
        functools.partial(restrict_kernel, geometry),
        grid=(steps,),
        in_specs=[
            pl.BlockSpec((chunk, width), lambda i: (i, 0)),
            row, row, row,
            pl.BlockSpec((kinds, order, order), lambda i: (0, 0, 0)),
            pl.BlockSpec((coarse, 16 * order), lambda i: (0, i)),
        ],
        out_specs=[
            pl.BlockSpec((coarse, width), lambda i: (0, 0)),
            pl.BlockSpec((4 * ghost, width), lambda i: (0, 0)),
            pl.BlockSpec((order, 16, coarse), lambda i: (0, i, 0)),
        ],
        out_shape=[
            jax.ShapeDtypeStruct((coarse, width), f32),
            jax.ShapeDtypeStruct((4 * ghost, width), bf16),
            jax.ShapeDtypeStruct((order, order, coarse), bf16),
        ],
        scratch_shapes=[
            pltpu.VMEM((kinds * width, width), bf16),
            pltpu.VMEM((8 * order, 8 * order), bf16),
            pltpu.VMEM((coarse + 4 * ghost, width), f32),
        ],
        compiler_params=pltpu.CompilerParams(vmem_limit_bytes=grant),
        name="restrict",
    )(fine_residual, owner, slot, kind, restrict_table, inverse_blocks)

    tiles = coarse // 128
    solved, returned = pl.pallas_call(
        functools.partial(
            coarse_kernel, (coarse, ghost, width, order, n_px, n_py, face_coef.shape[0])
        ),
        in_specs=[whole] * 5 + [pl.BlockSpec(memory_space=pltpu.SMEM)] + [whole] * 2,
        out_specs=[whole] * 2,
        out_shape=[
            jax.ShapeDtypeStruct((coarse, width), f32),
            jax.ShapeDtypeStruct((4 * ghost, width), bf16),
        ],
        scratch_shapes=[
            pltpu.VMEM((4 * ghost, width), bf16),
            pltpu.VMEM((4 * ghost, width), bf16),
            pltpu.VMEM((width, coarse), f32),
            pltpu.VMEM((width, coarse), f32),
            pltpu.VMEM((5, coarse, width), bf16),
            pltpu.VMEM((faces * coarse, 128), i32),
            pltpu.VMEM((faces * coarse, width), f32),
        ]
        + [pltpu.SemaphoreType.DMA((4,))] * 4
        + [pltpu.SemaphoreType.DMA((4, tiles))] * 2,
        compiler_params=pltpu.CompilerParams(
            collective_id=0, has_side_effects=True, vmem_limit_bytes=grant
        ),
        name="coarse",
    )(
        local, outgoing, ghost_slot.reshape(1, 4 * ghost), turned, face_table,
        face_coef.reshape(1, -1), coef_index, neighbours,
    )

    chunk = 512
    row = pl.BlockSpec((1, chunk), lambda i: (0, i))
    return pl.pallas_call(
        functools.partial(prolong_kernel, geometry),
        grid=(fine // chunk,),
        in_specs=[
            pl.BlockSpec((coarse, width), lambda i: (0, 0)),
            pl.BlockSpec((4 * ghost, width), lambda i: (0, 0)),
            row, row, row,
            pl.BlockSpec((kinds, order, order), lambda i: (0, 0, 0)),
        ],
        out_specs=[
            pl.BlockSpec((coarse, width), lambda i: (0, 0)),
            pl.BlockSpec((chunk, width), lambda i: (i, 0)),
        ],
        out_shape=[
            jax.ShapeDtypeStruct((coarse, width), f32),
            jax.ShapeDtypeStruct((fine, width), bf16),
        ],
        scratch_shapes=[
            pltpu.VMEM((kinds * width, width), bf16),
            pltpu.VMEM((coarse + 4 * ghost, width), bf16),
        ],
        compiler_params=pltpu.CompilerParams(vmem_limit_bytes=grant),
        name="prolong",
    )(solved, returned, owner, slot, kind, restrict_table)


def solution(mesh):
    both = ("px", "py")
    in_specs = (
        P(both, None), P(both), P(both), P(both, None), P(both), P(), P(both, None), P(), P(),
        P(None, both), P(None, both),
    )
    out_specs = (P(both, None), P(both, None))
    return jax.shard_map(
        functools.partial(shards, mesh.shape["px"], mesh.shape["py"]),
        mesh=mesh, in_specs=in_specs, out_specs=out_specs, check_vma=False,
    )
```

```python
import functools

import jax
import jax.numpy as jnp
from jax import lax
from jax.experimental import pallas as pl
from jax.experimental.pallas import tpu as pltpu
from jax.sharding import PartitionSpec as P

omega = 0.5
MESH = pl.DeviceIdType.MESH
f32 = jnp.float32
bf16 = jnp.bfloat16
i32 = jnp.int32
i16 = jnp.int16


def iota(shape, dim):
    return lax.broadcasted_iota(i32, shape, dim)


def nn(a, b):
    return lax.dot_general(a, b, (((1,), (0,)), ((), ())), preferred_element_type=f32)


def nt(a, b):
    return lax.dot_general(a, b, (((1,), (1,)), ((), ())), preferred_element_type=f32)


def onehot(mask):
    return jnp.where(mask, f32(1.0), f32(0.0)).astype(bf16)


def onehot16(left, right):
    return jnp.where(left == right, bf16(1.0), bf16(0.0))


def tiler(width, order):
    return onehot((iota((width, order), 0) & (order - 1)) == iota((width, order), 1))


def block_diagonal(matrix, width, flipped):
    order = matrix.shape[0]
    spread = tiler(width, order)
    if flipped:
        half = nt(spread, matrix)
    else:
        half = nn(spread, matrix)
    full = nt(half.astype(bf16), spread)
    bits = order.bit_length() - 1
    same = (iota((width, width), 0) >> bits) == (iota((width, width), 1) >> bits)
    return jnp.where(same, full, f32(0.0)).astype(bf16)


def columns_of(row):
    parts = [
        jnp.transpose(jnp.broadcast_to(row[:, at : at + 128], (128, 128)))
        for at in range(0, row.shape[1], 128)
    ]
    return jnp.concatenate(parts, axis=0)


def target_rows(owner, slot, me, coarse, ghost):
    offset = owner - me
    direction = jnp.where(offset == -1, 0, jnp.where(offset == 1, 1, jnp.where(offset < 0, 2, 3)))
    return jnp.where(offset == 0, slot, coarse + direction * ghost + slot)


def typed_sum(rows, kinds, tables, width, count):
    wide = jnp.concatenate([kinds.astype(i16)] * (width // 128), axis=1)
    parts = [jnp.where(wide == i16(kind), rows, bf16(0.0)) for kind in range(count)]
    return nn(jnp.concatenate(parts, axis=1), tables[...])


def restrict_kernel(
    geometry, fine_ref, owner_ref, slot_ref, kind_ref, table_ref,
    local_ref, out_ref, tables, total,
):
    coarse, ghost, width, order, kinds, n_py = geometry
    me = lax.axis_index("px") * n_py + lax.axis_index("py")
    step = pl.program_id(0)

    @pl.when(step == 0)
    def _():
        for kind in range(kinds):
            tables[kind * width : (kind + 1) * width, :] = block_diagonal(
                table_ref[kind], width, True
            )
        total[...] = jnp.zeros_like(total)

    chunk = fine_ref.shape[0]
    for begin in range(0, chunk, 512):
        span = slice(begin, begin + 512)
        contrib = typed_sum(
            fine_ref[span, :], columns_of(kind_ref[:, span]), tables, width, kinds
        ).astype(bf16)
        target = target_rows(owner_ref[:, span], slot_ref[:, span], me, coarse, ghost)
        rows = coarse + 4 * ghost
        picks = onehot16(iota((rows, 512), 0).astype(i16), target.astype(i16))
        total[...] += nn(picks, contrib)

    @pl.when(step == pl.num_programs(0) - 1)
    def _():
        local_ref[...] = total[:coarse, :]
        out_ref[...] = total[coarse:, :].astype(bf16)


def coarse_kernel(
    geometry, local_ref, outgoing, ghost_row_ref, inverse_ref, face_ref, coef_ref, index_ref,
    neighbour_ref, table_ref, solution_ref, returned, tables_ref,
    blocks, turned, perm, couplings, block_sem, incoming, reply, xt, first_t, near, code, beside,
    ghost_send, ghost_recv, reply_send, reply_recv, halo_send, halo_recv,
):
    coarse, ghost, width, order, n_px, n_py, kinds = geometry
    rhs = width // order
    faces = face_ref.shape[0]
    px = lax.axis_index("px")
    py = lax.axis_index("py")
    me = px * n_py + py
    fetch = pltpu.make_async_copy(inverse_ref, blocks, block_sem)
    fetch.start()
    exists = [py > 0, py < n_py - 1, px > 0, px < n_px - 1]
    place = [(px, py - 1), (px, py + 1), (px - 1, py), (px + 1, py)]
    far = [(py > 1, (px, py - 2)), (py < n_py - 2, (px, py + 2))]

    for slot, there in enumerate(exists):
        @pl.when(jnp.logical_not(there))
        def _():
            near[slot + 1] = jnp.zeros((coarse, width), bf16)
            incoming[pl.ds(slot * ghost, ghost), :] = jnp.zeros((ghost, width), bf16)
            returned[pl.ds(slot * ghost, ghost), :] = jnp.zeros((ghost, width), bf16)

    barrier = pltpu.get_barrier_semaphore()
    everyone = list(zip(exists, place)) + far
    for there, where in everyone:
        @pl.when(there)
        def _():
            pl.semaphore_signal(barrier, inc=1, device_id=where, device_id_type=MESH)
    pl.semaphore_wait(barrier, sum(there.astype(i32) for there, _ in everyone))

    def lists(source, target, send, recv, at, to):
        return pltpu.make_async_remote_copy(
            src_ref=source.at[pl.ds(at * ghost, ghost)],
            dst_ref=target.at[pl.ds(to * ghost, ghost)],
            send_sem=send.at[at],
            recv_sem=recv.at[to],
            device_id=place[at],
            device_id_type=MESH,
        )

    def start_lists(source, target, send, recv):
        for at in range(4):
            @pl.when(exists[at])
            def _():
                lists(source, target, send, recv, at, at ^ 1).start()

    def finish_lists(source, target, send, recv):
        for at in range(4):
            @pl.when(exists[at])
            def _():
                lists(source, target, send, recv, at, at).wait_recv()
                lists(source, target, send, recv, at, at ^ 1).wait_send()

    start_lists(outgoing, incoming, ghost_send, ghost_recv)

    half = 8 * order
    at = iota((half, half), 0)
    perm[...] = onehot(iota((half, half), 1) == (at & 7) * order + (at >> 3))
    for face in range(faces):
        couplings[face] = block_diagonal(face_ref[face], width, False)
    offset = lax.shift_right_logical(neighbour_ref[...], coarse.bit_length() - 1) - me
    slot = jnp.where(
        offset == 0, 0,
        jnp.where(offset == -1, 1, jnp.where(offset == 1, 2, jnp.where(offset < 0, 3, 4))),
    )
    codes = slot * coarse + (neighbour_ref[...] & (coarse - 1))
    for face in range(faces):
        code[face * coarse : (face + 1) * coarse, :] = columns_of(codes[face : face + 1, :])
    scales = jnp.zeros(index_ref.shape, f32)
    for kind in range(kinds):
        scales = jnp.where(index_ref[...] == kind, coef_ref[0, kind], scales)
    lists_onehot = onehot(iota((coarse, 4 * ghost), 0) == ghost_row_ref[...])
    pick_onehot = onehot(
        jnp.concatenate([columns_of(ghost_row_ref[...])] * (coarse // 128), axis=1)
        == iota((4 * ghost, coarse), 1)
    )

    fetch.wait()

    def turn(group, _):
        halves = [
            nt(
                perm[...], blocks[:, pl.ds(pl.multiple_of((2 * group + at) * half, half), half)]
            ).reshape(order, 8, coarse)
            for at in range(2)
        ]
        rows = pl.ds(pl.multiple_of(group * 16, 16), 16)
        turned[:, rows, :] = jnp.concatenate(halves, axis=1).astype(bf16)
        return 0

    lax.fori_loop(0, order // 16, turn, 0)

    finish_lists(outgoing, incoming, ghost_send, ghost_recv)
    rhs_rows = local_ref[...] + nn(lists_onehot, incoming[...])
    xt[...] = jnp.transpose(rhs_rows.astype(bf16).astype(f32))

    def sweep(tile):
        lanes = slice(tile * 128, (tile + 1) * 128)

        def body(block, sums):
            sums = list(sums)
            values = [
                xt[pl.ds(pl.multiple_of(s * order + block * 8, 8), 8), lanes] for s in range(rhs)
            ]
            for inner in range(8):
                at = block * 8 + inner
                matrix = turned[at, :, lanes].astype(f32)
                for s in range(rhs):
                    sums[s] = sums[s] + matrix * values[s][inner : inner + 1, :]
            return tuple(sums)

        start = tuple(jnp.zeros((order, 128), f32) for _ in range(rhs))
        return jnp.concatenate(lax.fori_loop(0, order // 8, body, start), axis=0)

    even = lax.rem(py, 2) == 0
    partner = jnp.where(even, 2, 1)
    beyond = 3 - partner
    partner_place = (px, jnp.where(even, py + 1, py - 1))
    relay_place = (px, jnp.where(even, py + 2, py - 2))
    relays = jnp.where(even, py + 2, n_py + 1 - py) < n_py
    gets_relay = jnp.where(even, py - 2, n_py - 3 - py) >= 0

    def halo(role, tile, source, target, where):
        rows = pl.ds(tile * 128, 128)
        return pltpu.make_async_remote_copy(
            src_ref=near.at[source, rows],
            dst_ref=near.at[target, rows],
            send_sem=halo_send.at[role, tile],
            recv_sem=halo_recv.at[role, tile],
            device_id=where,
            device_id_type=MESH,
        )

    def to_partner(tile):
        return halo(0, tile, 0, beyond, partner_place)

    def from_partner(tile):
        return halo(0, tile, 0, partner, partner_place)

    def onward(tile):
        return halo(1, tile, partner, beyond, relay_place)

    def from_relay(tile):
        return halo(1, tile, partner, beyond, relay_place)

    def lower(tile):
        return halo(2, tile, 0, 4, place[2])

    def upper(tile):
        return halo(3, tile, 0, 3, place[3])

    tiles = coarse // 128
    for tile in range(tiles):
        lanes = slice(tile * 128, (tile + 1) * 128)
        rounded = sweep(tile).astype(bf16).astype(f32)
        first_t[:, lanes] = rounded
        near[0, lanes, :] = jnp.transpose(rounded).astype(bf16)
        to_partner(tile).start()

        @pl.when(exists[2])
        def _():
            lower(tile).start()

        @pl.when(exists[3])
        def _():
            upper(tile).start()

    step_rows = coarse
    steps = faces * coarse // step_rows

    def gather(block, begin, end, fresh):
        def body(step, _):
            rows = pl.ds(pl.multiple_of(step * step_rows, step_rows), step_rows)
            here = (code[rows, :] - block * coarse).astype(i16)
            lane = iota((step_rows, 128), 1).astype(i16)
            picks = jnp.concatenate(
                [onehot16(here - i16(at * 128), lane) for at in range(tiles)], axis=1
            )
            found = nn(picks, near[block])
            if fresh:
                beside[rows, :] = found
            else:
                beside[rows, :] += found
            return 0

        lax.fori_loop(begin, end, body, 0)

    for tile in range(tiles):
        from_partner(tile).wait_recv()

        @pl.when(relays)
        def _():
            onward(tile).start()
        gather(0, tile * steps // tiles, (tile + 1) * steps // tiles, True)
    gather(partner, 0, steps, False)

    @pl.when(exists[2])
    def _():
        for tile in range(tiles):
            halo(3, tile, 0, 3, place[2]).wait_recv()
    gather(3, 0, steps, False)

    @pl.when(exists[3])
    def _():
        for tile in range(tiles):
            halo(2, tile, 0, 4, place[3]).wait_recv()
    gather(4, 0, steps, False)

    @pl.when(gets_relay)
    def _():
        for tile in range(tiles):
            from_relay(tile).wait_recv()
    gather(beyond, 0, steps, False)

    coupled = jnp.zeros((width, coarse), f32)
    for face in range(faces):
        rows = slice(face * coarse, (face + 1) * coarse)
        coupled += nt(couplings[face], beside[rows, :].astype(bf16)) * scales[face : face + 1, :]
    xt[...] = coupled.astype(bf16).astype(f32)

    for tile in range(tiles):
        lanes = slice(tile * 128, (tile + 1) * 128)
        solved = first_t[:, lanes] - omega * sweep(tile)
        solution_ref[lanes, :] = jnp.transpose(solved)

    reply[...] = nn(pick_onehot, solution_ref[...].astype(bf16)).astype(bf16)
    start_lists(reply, returned, reply_send, reply_recv)
    for kind in range(table_ref.shape[0]):
        tables_ref[kind * width : (kind + 1) * width, :] = block_diagonal(
            table_ref[kind], width, False
        )
    for tile in range(tiles):
        to_partner(tile).wait_send()

        @pl.when(relays)
        def _():
            onward(tile).wait_send()

        @pl.when(exists[2])
        def _():
            lower(tile).wait_send()

        @pl.when(exists[3])
        def _():
            upper(tile).wait_send()
    finish_lists(reply, returned, reply_send, reply_recv)


def prolong_kernel(
    geometry, solution_ref, returned_ref, owner_ref, slot_ref, kind_ref, tables,
    out_solution_ref, fine_ref, held,
):
    coarse, ghost, width, order, kinds, n_py = geometry
    me = lax.axis_index("px") * n_py + lax.axis_index("py")
    step = pl.program_id(0)

    @pl.when(step == 0)
    def _():
        held[:coarse, :] = solution_ref[...].astype(bf16)
        held[coarse:, :] = returned_ref[...]
        out_solution_ref[...] = solution_ref[...]

    rows = coarse + 4 * ghost
    target = columns_of(target_rows(owner_ref[...], slot_ref[...], me, coarse, ghost))
    target = target.astype(i16)
    lane = iota(target.shape, 1).astype(i16)
    picks = jnp.concatenate(
        [onehot16(target - i16(at), lane) for at in range(0, rows, 128)], axis=1
    )
    fetched = nn(picks, held[...]).astype(bf16)
    fine_ref[...] = typed_sum(
        fetched, columns_of(kind_ref[...]), tables, width, kinds
    ).astype(bf16)


def shards(
    n_px, n_py,
    fine_residual, dest_owner, coarse_slot, ghost_slot, child_type, restrict_table,
    inverse_blocks, face_table, face_coef, coef_index, neighbours,
):
    fine, width = fine_residual.shape
    coarse = inverse_blocks.shape[0]
    ghost = ghost_slot.shape[1]
    kinds, order, _ = restrict_table.shape
    faces = face_table.shape[0]
    owner = dest_owner.reshape(1, fine)
    slot = coarse_slot.reshape(1, fine)
    kind = child_type.reshape(1, fine)
    whole = pl.BlockSpec(memory_space=pltpu.VMEM)
    grant = 48 * 1024 * 1024

    chunk = 1024
    geometry = (coarse, ghost, width, order, kinds, n_py)
    row = pl.BlockSpec((1, chunk), lambda i: (0, i))
    local, outgoing = pl.pallas_call(
        functools.partial(restrict_kernel, geometry),
        grid=(fine // chunk,),
        in_specs=[
            pl.BlockSpec((chunk, width), lambda i: (i, 0)),
            row, row, row,
            pl.BlockSpec((kinds, order, order), lambda i: (0, 0, 0)),
        ],
        out_specs=[
            pl.BlockSpec((coarse, width), lambda i: (0, 0)),
            pl.BlockSpec((4 * ghost, width), lambda i: (0, 0)),
        ],
        out_shape=[
            jax.ShapeDtypeStruct((coarse, width), f32),
            jax.ShapeDtypeStruct((4 * ghost, width), bf16),
        ],
        scratch_shapes=[
            pltpu.VMEM((kinds * width, width), bf16),
            pltpu.VMEM((coarse + 4 * ghost, width), f32),
        ],
        compiler_params=pltpu.CompilerParams(vmem_limit_bytes=63400000),
        name="restrict",
    )(fine_residual, owner, slot, kind, restrict_table)

    tiles = coarse // 128
    solved, returned, tables = pl.pallas_call(
        functools.partial(
            coarse_kernel, (coarse, ghost, width, order, n_px, n_py, face_coef.shape[0])
        ),
        in_specs=[whole] * 3
        + [pl.BlockSpec(memory_space=pl.ANY), whole, pl.BlockSpec(memory_space=pltpu.SMEM)]
        + [whole] * 3,
        out_specs=[whole] * 3,
        out_shape=[
            jax.ShapeDtypeStruct((coarse, width), f32),
            jax.ShapeDtypeStruct((4 * ghost, width), bf16),
            jax.ShapeDtypeStruct((kinds * width, width), bf16),
        ],
        scratch_shapes=[
            pltpu.VMEM(inverse_blocks.shape, bf16),
            pltpu.VMEM((order, order, coarse), bf16),
            pltpu.VMEM((8 * order, 8 * order), bf16),
            pltpu.VMEM((faces, width, width), bf16),
            pltpu.SemaphoreType.DMA,
            pltpu.VMEM((4 * ghost, width), bf16),
            pltpu.VMEM((4 * ghost, width), bf16),
            pltpu.VMEM((width, coarse), f32),
            pltpu.VMEM((width, coarse), f32),
            pltpu.VMEM((5, coarse, width), bf16),
            pltpu.VMEM((faces * coarse, 128), i32),
            pltpu.VMEM((faces * coarse, width), f32),
        ]
        + [pltpu.SemaphoreType.DMA((4,))] * 4
        + [pltpu.SemaphoreType.DMA((4, tiles))] * 2,
        compiler_params=pltpu.CompilerParams(
            collective_id=0, has_side_effects=True, vmem_limit_bytes=grant
        ),
        name="coarse",
    )(
        local, outgoing, ghost_slot.reshape(1, 4 * ghost), inverse_blocks, face_table,
        face_coef.reshape(1, -1), coef_index, neighbours, restrict_table,
    )

    chunk = 512
    row = pl.BlockSpec((1, chunk), lambda i: (0, i))
    return pl.pallas_call(
        functools.partial(prolong_kernel, geometry),
        grid=(fine // chunk,),
        in_specs=[
            pl.BlockSpec((coarse, width), lambda i: (0, 0)),
            pl.BlockSpec((4 * ghost, width), lambda i: (0, 0)),
            row, row, row,
            pl.BlockSpec((kinds * width, width), lambda i: (0, 0)),
        ],
        out_specs=[
            pl.BlockSpec((coarse, width), lambda i: (0, 0)),
            pl.BlockSpec((chunk, width), lambda i: (i, 0)),
        ],
        out_shape=[
            jax.ShapeDtypeStruct((coarse, width), f32),
            jax.ShapeDtypeStruct((fine, width), bf16),
        ],
        scratch_shapes=[
            pltpu.VMEM((coarse + 4 * ghost, width), bf16),
        ],
        compiler_params=pltpu.CompilerParams(vmem_limit_bytes=grant),
        name="prolong",
    )(solved, returned, owner, slot, kind, tables)


def solution(mesh):
    both = ("px", "py")
    in_specs = (
        P(both, None), P(both), P(both), P(both, None), P(both), P(), P(both, None), P(), P(),
        P(None, both), P(None, both),
    )
    out_specs = (P(both, None), P(both, None))
    return jax.shard_map(
        functools.partial(shards, mesh.shape["px"], mesh.shape["py"]),
        mesh=mesh, in_specs=in_specs, out_specs=out_specs, check_vma=False,
    )
```

```python
import functools

import jax
import jax.numpy as jnp
from jax import lax
from jax.experimental import pallas as pl
from jax.experimental.pallas import tpu as pltpu
from jax.sharding import PartitionSpec as P

omega = 0.5
MESH = pl.DeviceIdType.MESH
f32 = jnp.float32
bf16 = jnp.bfloat16
i32 = jnp.int32
i16 = jnp.int16


def iota(shape, dim):
    return lax.broadcasted_iota(i32, shape, dim)


def nn(a, b):
    return lax.dot_general(a, b, (((1,), (0,)), ((), ())), preferred_element_type=f32)


def nt(a, b):
    return lax.dot_general(a, b, (((1,), (1,)), ((), ())), preferred_element_type=f32)


def onehot(mask):
    return jnp.where(mask, f32(1.0), f32(0.0)).astype(bf16)


def onehot16(left, right):
    return jnp.where(left == right, bf16(1.0), bf16(0.0))


def tiler(width, order):
    return onehot((iota((width, order), 0) & (order - 1)) == iota((width, order), 1))


def block_diagonal(matrix, width, flipped):
    order = matrix.shape[0]
    spread = tiler(width, order)
    if flipped:
        half = nt(spread, matrix)
    else:
        half = nn(spread, matrix)
    full = nt(half.astype(bf16), spread)
    bits = order.bit_length() - 1
    same = (iota((width, width), 0) >> bits) == (iota((width, width), 1) >> bits)
    return jnp.where(same, full, f32(0.0)).astype(bf16)


def columns_of(row):
    parts = [
        jnp.transpose(jnp.broadcast_to(row[:, at : at + 128], (128, 128)))
        for at in range(0, row.shape[1], 128)
    ]
    return jnp.concatenate(parts, axis=0)


def target_rows(owner, slot, me, coarse, ghost):
    offset = owner - me
    direction = jnp.where(offset == -1, 0, jnp.where(offset == 1, 1, jnp.where(offset < 0, 2, 3)))
    return jnp.where(offset == 0, slot, coarse + direction * ghost + slot)


def typed_sum(rows, kinds, tables, width, count):
    wide = jnp.concatenate([kinds.astype(i16)] * (width // 128), axis=1)
    parts = [jnp.where(wide == i16(kind), rows, bf16(0.0)) for kind in range(count)]
    return nn(jnp.concatenate(parts, axis=1), tables[...])


def restrict_kernel(
    geometry, fine_ref, owner_ref, slot_ref, kind_ref, table_ref,
    local_ref, out_ref, tables, total,
):
    coarse, ghost, width, order, kinds, n_py = geometry
    me = lax.axis_index("px") * n_py + lax.axis_index("py")
    step = pl.program_id(0)

    @pl.when(step == 0)
    def _():
        for kind in range(kinds):
            tables[kind * width : (kind + 1) * width, :] = block_diagonal(
                table_ref[kind], width, True
            )
        total[...] = jnp.zeros_like(total)

    chunk = fine_ref.shape[0]
    for begin in range(0, chunk, 512):
        span = slice(begin, begin + 512)
        contrib = typed_sum(
            fine_ref[span, :], columns_of(kind_ref[:, span]), tables, width, kinds
        ).astype(bf16)
        target = target_rows(owner_ref[:, span], slot_ref[:, span], me, coarse, ghost)
        rows = coarse + 4 * ghost
        picks = onehot16(iota((rows, 512), 0).astype(i16), target.astype(i16))
        total[...] += nn(picks, contrib)

    @pl.when(step == pl.num_programs(0) - 1)
    def _():
        local_ref[...] = total[:coarse, :]
        out_ref[...] = total[coarse:, :].astype(bf16)


def coarse_kernel(
    geometry, sums_ref, outgoing, ghost_ref, inverse_ref, face_ref, coef_ref, index_ref,
    neighbour_ref, table_ref, solution_ref, returned, tables_ref,
    blocks, local_ref, turned, perm, couplings, block_sem, sums_sem, incoming, reply, xt, first_t, near, code, beside,
    ghost_send, ghost_recv, reply_send, reply_recv, halo_send, halo_recv,
):
    coarse, ghost, width, order, n_px, n_py, kinds = geometry
    rhs = width // order
    faces = face_ref.shape[0]
    px = lax.axis_index("px")
    py = lax.axis_index("py")
    me = px * n_py + py
    fetch = pltpu.make_async_copy(inverse_ref, blocks, block_sem)
    fetch.start()
    fetch_sums = pltpu.make_async_copy(sums_ref, local_ref, sums_sem)
    fetch_sums.start()
    exists = [py > 0, py < n_py - 1, px > 0, px < n_px - 1]
    place = [(px, py - 1), (px, py + 1), (px - 1, py), (px + 1, py)]
    far = [(py > 1, (px, py - 2)), (py < n_py - 2, (px, py + 2))]

    for slot, there in enumerate(exists):
        @pl.when(jnp.logical_not(there))
        def _():
            near[slot + 1] = jnp.zeros((coarse, width), bf16)
            incoming[pl.ds(slot * ghost, ghost), :] = jnp.zeros((ghost, width), bf16)
            returned[pl.ds(slot * ghost, ghost), :] = jnp.zeros((ghost, width), bf16)

    barrier = pltpu.get_barrier_semaphore()
    everyone = list(zip(exists, place)) + far
    for there, where in everyone:
        @pl.when(there)
        def _():
            pl.semaphore_signal(barrier, inc=1, device_id=where, device_id_type=MESH)
    pl.semaphore_wait(barrier, sum(there.astype(i32) for there, _ in everyone))

    def lists(source, target, send, recv, at, to):
        return pltpu.make_async_remote_copy(
            src_ref=source.at[pl.ds(at * ghost, ghost)],
            dst_ref=target.at[pl.ds(to * ghost, ghost)],
            send_sem=send.at[at],
            recv_sem=recv.at[to],
            device_id=place[at],
            device_id_type=MESH,
        )

    def start_lists(source, target, send, recv):
        for at in range(4):
            @pl.when(exists[at])
            def _():
                lists(source, target, send, recv, at, at ^ 1).start()

    def finish_lists(source, target, send, recv):
        for at in range(4):
            @pl.when(exists[at])
            def _():
                lists(source, target, send, recv, at, at).wait_recv()
                lists(source, target, send, recv, at, at ^ 1).wait_send()

    start_lists(outgoing, incoming, ghost_send, ghost_recv)

    half = 8 * order
    at = iota((half, half), 0)
    perm[...] = onehot(iota((half, half), 1) == (at & 7) * order + (at >> 3))
    for face in range(faces):
        couplings[face] = block_diagonal(face_ref[face], width, False)
    offset = lax.shift_right_logical(neighbour_ref[...], coarse.bit_length() - 1) - me
    slot = jnp.where(
        offset == 0, 0,
        jnp.where(offset == -1, 1, jnp.where(offset == 1, 2, jnp.where(offset < 0, 3, 4))),
    )
    codes = slot * coarse + (neighbour_ref[...] & (coarse - 1))
    for face in range(faces):
        code[face * coarse : (face + 1) * coarse, :] = columns_of(
            codes[face : face + 1, :]
        ).astype(i16)
    scales = jnp.zeros(index_ref.shape, f32)
    for kind in range(kinds):
        scales = jnp.where(index_ref[...] == kind, coef_ref[0, kind], scales)
    ghost_row = jnp.concatenate([ghost_ref[at : at + 1, :] for at in range(4)], axis=1)
    lists_onehot = onehot(iota((coarse, 4 * ghost), 0) == ghost_row)
    pick_onehot = onehot(
        jnp.concatenate([columns_of(ghost_row)] * (coarse // 128), axis=1)
        == iota((4 * ghost, coarse), 1)
    )

    fetch.wait()
    fetch_sums.wait()

    def turn(group, _):
        halves = [
            nt(
                perm[...], blocks[:, pl.ds(pl.multiple_of((2 * group + at) * half, half), half)]
            ).reshape(order, 8, coarse)
            for at in range(2)
        ]
        rows = pl.ds(pl.multiple_of(group * 16, 16), 16)
        turned[:, rows, :] = jnp.concatenate(halves, axis=1).astype(bf16)
        return 0

    lax.fori_loop(0, order // 16, turn, 0)

    finish_lists(outgoing, incoming, ghost_send, ghost_recv)
    rhs_rows = local_ref[...] + nn(lists_onehot, incoming[...])
    xt[...] = jnp.transpose(rhs_rows.astype(bf16).astype(f32))

    def sweep(tile):
        lanes = slice(tile * 128, (tile + 1) * 128)

        def body(block, sums):
            sums = list(sums)
            values = [
                xt[pl.ds(pl.multiple_of(s * order + block * 8, 8), 8), lanes] for s in range(rhs)
            ]
            for inner in range(8):
                at = block * 8 + inner
                matrix = turned[at, :, lanes].astype(f32)
                for s in range(rhs):
                    sums[s] = sums[s] + matrix * values[s][inner : inner + 1, :]
            return tuple(sums)

        start = tuple(jnp.zeros((order, 128), f32) for _ in range(rhs))
        return jnp.concatenate(lax.fori_loop(0, order // 8, body, start), axis=0)

    even = lax.rem(py, 2) == 0
    partner = jnp.where(even, 2, 1)
    beyond = 3 - partner
    partner_place = (px, jnp.where(even, py + 1, py - 1))
    relay_place = (px, jnp.where(even, py + 2, py - 2))
    relays = jnp.where(even, py + 2, n_py + 1 - py) < n_py
    gets_relay = jnp.where(even, py - 2, n_py - 3 - py) >= 0

    def halo(role, tile, source, target, where):
        rows = pl.ds(tile * 128, 128)
        return pltpu.make_async_remote_copy(
            src_ref=near.at[source, rows],
            dst_ref=near.at[target, rows],
            send_sem=halo_send.at[role, tile],
            recv_sem=halo_recv.at[role, tile],
            device_id=where,
            device_id_type=MESH,
        )

    def to_partner(tile):
        return halo(0, tile, 0, beyond, partner_place)

    def from_partner(tile):
        return halo(0, tile, 0, partner, partner_place)

    def onward(tile):
        return halo(1, tile, partner, beyond, relay_place)

    def from_relay(tile):
        return halo(1, tile, partner, beyond, relay_place)

    def lower(tile):
        return halo(2, tile, 0, 4, place[2])

    def upper(tile):
        return halo(3, tile, 0, 3, place[3])

    tiles = coarse // 128
    for tile in range(tiles):
        lanes = slice(tile * 128, (tile + 1) * 128)
        rounded = sweep(tile).astype(bf16).astype(f32)
        first_t[:, lanes] = rounded
        near[0, lanes, :] = jnp.transpose(rounded).astype(bf16)
        to_partner(tile).start()

        @pl.when(exists[2])
        def _():
            lower(tile).start()

        @pl.when(exists[3])
        def _():
            upper(tile).start()

    def picked(face, block):
        rows = pl.ds(pl.multiple_of(face * coarse, coarse), coarse)
        here = code[rows, :] - jnp.asarray(block * coarse, i32).astype(i16)
        lane = iota((coarse, 128), 1).astype(i16)
        picks = jnp.concatenate(
            [onehot16(here - i16(at * 128), lane) for at in range(tiles)], axis=1
        )
        return nn(picks, near[block])

    def own_pass(face, _):
        rows = pl.ds(pl.multiple_of(face * coarse, coarse), coarse)
        beside[rows, :] = picked(face, 0).astype(bf16)
        return 0

    def middle_pass(face, _):
        rows = pl.ds(pl.multiple_of(face * coarse, coarse), coarse)
        found = picked(face, 3) + picked(face, 4) + picked(face, partner)
        beside[rows, :] += found.astype(bf16)
        return 0

    for tile in range(tiles):
        from_partner(tile).wait_recv()

        @pl.when(relays)
        def _():
            onward(tile).start()
        lax.fori_loop(tile * faces // tiles, (tile + 1) * faces // tiles, own_pass, 0)

    @pl.when(exists[2])
    def _():
        for tile in range(tiles):
            halo(3, tile, 0, 3, place[2]).wait_recv()

    @pl.when(exists[3])
    def _():
        for tile in range(tiles):
            halo(2, tile, 0, 4, place[3]).wait_recv()
    lax.fori_loop(0, faces, middle_pass, 0)

    @pl.when(gets_relay)
    def _():
        for tile in range(tiles):
            from_relay(tile).wait_recv()

    coupled = jnp.zeros((width, coarse), f32)
    for face in range(faces):
        rows = slice(face * coarse, (face + 1) * coarse)
        found = beside[rows, :] + picked(face, beyond).astype(bf16)
        coupled += nt(couplings[face], found) * scales[face : face + 1, :]
    xt[...] = coupled.astype(bf16).astype(f32)

    for tile in range(tiles):
        lanes = slice(tile * 128, (tile + 1) * 128)
        solved = first_t[:, lanes] - omega * sweep(tile)
        solution_ref[lanes, :] = jnp.transpose(solved)

    reply[...] = nn(pick_onehot, solution_ref[...].astype(bf16)).astype(bf16)
    start_lists(reply, returned, reply_send, reply_recv)
    for kind in range(table_ref.shape[0]):
        tables_ref[kind * width : (kind + 1) * width, :] = block_diagonal(
            table_ref[kind], width, False
        )
    for tile in range(tiles):
        to_partner(tile).wait_send()

        @pl.when(relays)
        def _():
            onward(tile).wait_send()

        @pl.when(exists[2])
        def _():
            lower(tile).wait_send()

        @pl.when(exists[3])
        def _():
            upper(tile).wait_send()
    finish_lists(reply, returned, reply_send, reply_recv)


def prolong_kernel(
    geometry, solution_ref, returned_ref, owner_ref, slot_ref, kind_ref, tables,
    out_solution_ref, fine_ref, held,
):
    coarse, ghost, width, order, kinds, n_py = geometry
    me = lax.axis_index("px") * n_py + lax.axis_index("py")
    step = pl.program_id(0)

    @pl.when(step == 0)
    def _():
        held[:coarse, :] = solution_ref[...].astype(bf16)
        held[coarse:, :] = returned_ref[...]
        out_solution_ref[...] = solution_ref[...]

    rows = coarse + 4 * ghost
    for begin in range(0, fine_ref.shape[0], 512):
        span = slice(begin, begin + 512)
        target = columns_of(
            target_rows(owner_ref[:, span], slot_ref[:, span], me, coarse, ghost)
        ).astype(i16)
        lane = iota(target.shape, 1).astype(i16)
        picks = jnp.concatenate(
            [onehot16(target - i16(at), lane) for at in range(0, rows, 128)], axis=1
        )
        fetched = nn(picks, held[...]).astype(bf16)
        fine_ref[span, :] = typed_sum(
            fetched, columns_of(kind_ref[:, span]), tables, width, kinds
        ).astype(bf16)


def shards(
    n_px, n_py,
    fine_residual, dest_owner, coarse_slot, ghost_slot, child_type, restrict_table,
    inverse_blocks, face_table, face_coef, coef_index, neighbours,
):
    fine, width = fine_residual.shape
    coarse = inverse_blocks.shape[0]
    ghost = ghost_slot.shape[1]
    kinds, order, _ = restrict_table.shape
    faces = face_table.shape[0]
    owner = dest_owner.reshape(1, fine)
    slot = coarse_slot.reshape(1, fine)
    kind = child_type.reshape(1, fine)
    whole = pl.BlockSpec(memory_space=pltpu.VMEM)
    grant = 48 * 1024 * 1024

    chunk = 1024
    geometry = (coarse, ghost, width, order, kinds, n_py)
    row = pl.BlockSpec((1, chunk), lambda i: (0, i))
    local, outgoing = pl.pallas_call(
        functools.partial(restrict_kernel, geometry),
        grid=(fine // chunk,),
        in_specs=[
            pl.BlockSpec((chunk, width), lambda i: (i, 0)),
            row, row, row,
            pl.BlockSpec((kinds, order, order), lambda i: (0, 0, 0)),
        ],
        out_specs=[
            pl.BlockSpec((coarse, width), lambda i: (0, 0)),
            pl.BlockSpec((4 * ghost, width), lambda i: (0, 0)),
        ],
        out_shape=[
            jax.ShapeDtypeStruct((coarse, width), f32),
            jax.ShapeDtypeStruct((4 * ghost, width), bf16),
        ],
        scratch_shapes=[
            pltpu.VMEM((kinds * width, width), bf16),
            pltpu.VMEM((coarse + 4 * ghost, width), f32),
        ],
        compiler_params=pltpu.CompilerParams(vmem_limit_bytes=63400000),
        name="restrict",
    )(fine_residual, owner, slot, kind, restrict_table)

    tiles = coarse // 128
    solved, returned, tables = pl.pallas_call(
        functools.partial(
            coarse_kernel, (coarse, ghost, width, order, n_px, n_py, face_coef.shape[0])
        ),
        in_specs=[pl.BlockSpec(memory_space=pltpu.HBM)] * 2
        + [whole, pl.BlockSpec(memory_space=pltpu.HBM), whole, pl.BlockSpec(memory_space=pltpu.SMEM)]
        + [whole] * 3,
        out_specs=[whole] * 3,
        out_shape=[
            jax.ShapeDtypeStruct((coarse, width), f32),
            jax.ShapeDtypeStruct((4 * ghost, width), bf16),
            jax.ShapeDtypeStruct((kinds * width, width), bf16),
        ],
        scratch_shapes=[
            pltpu.VMEM(inverse_blocks.shape, bf16),
            pltpu.VMEM((coarse, width), f32),
            pltpu.VMEM((order, order, coarse), bf16),
            pltpu.VMEM((8 * order, 8 * order), bf16),
            pltpu.VMEM((faces, width, width), bf16),
            pltpu.SemaphoreType.DMA,
            pltpu.SemaphoreType.DMA,
            pltpu.VMEM((4 * ghost, width), bf16),
            pltpu.VMEM((4 * ghost, width), bf16),
            pltpu.VMEM((width, coarse), f32),
            pltpu.VMEM((width, coarse), f32),
            pltpu.VMEM((5, coarse, width), bf16),
            pltpu.VMEM((faces * coarse, 128), i16),
            pltpu.VMEM((faces * coarse, width), bf16),
        ]
        + [pltpu.SemaphoreType.DMA((4,))] * 4
        + [pltpu.SemaphoreType.DMA((4, tiles))] * 2,
        compiler_params=pltpu.CompilerParams(
            collective_id=0, has_side_effects=True, vmem_limit_bytes=grant
        ),
        name="coarse",
    )(
        local, outgoing, ghost_slot, inverse_blocks, face_table,
        face_coef.reshape(1, -1), coef_index, neighbours, restrict_table,
    )

    chunk = 1024
    row = pl.BlockSpec((1, chunk), lambda i: (0, i))
    return pl.pallas_call(
        functools.partial(prolong_kernel, geometry),
        grid=(fine // chunk,),
        in_specs=[
            pl.BlockSpec((coarse, width), lambda i: (0, 0)),
            pl.BlockSpec((4 * ghost, width), lambda i: (0, 0)),
            row, row, row,
            pl.BlockSpec((kinds * width, width), lambda i: (0, 0)),
        ],
        out_specs=[
            pl.BlockSpec((coarse, width), lambda i: (0, 0)),
            pl.BlockSpec((chunk, width), lambda i: (i, 0)),
        ],
        out_shape=[
            jax.ShapeDtypeStruct((coarse, width), f32),
            jax.ShapeDtypeStruct((fine, width), bf16),
        ],
        scratch_shapes=[
            pltpu.VMEM((coarse + 4 * ghost, width), bf16),
        ],
        compiler_params=pltpu.CompilerParams(vmem_limit_bytes=grant),
        name="prolong",
    )(solved, returned, owner, slot, kind, tables)


def solution(mesh):
    both = ("px", "py")
    in_specs = (
        P(both, None), P(both), P(both), P(both, None), P(both), P(), P(both, None), P(), P(),
        P(None, both), P(None, both),
    )
    out_specs = (P(both, None), P(both, None))
    return jax.shard_map(
        functools.partial(shards, mesh.shape["px"], mesh.shape["py"]),
        mesh=mesh, in_specs=in_specs, out_specs=out_specs, check_vma=False,
    )
```
